32 devices in a mesh: mem: 8 (over y, x, core), slab: 4 (over z).
Axes of the slice: x: 2, y: 2, z: 4, core: 2. Of those that a mesh axis runs over, the one named last changes fastest.
Arguments:
- prior_sample_stack: float32 [8, 3, 16, 512], P('mem', None, None, 'slab'), may hold values from -4 to 4
- obs_cell: int32 [8, 512], P('mem', 'slab'), may hold values from 0 to 255
- obs_value: float32 [8, 512], P('mem', 'slab'), may hold values from -4 to 4
- obs_bin: int32 [8, 512], P('mem', 'slab'), may hold values from 0 to 3
Outputs:
- analysis: float32 [8, 3, 16, 512], P('mem', None, None, 'slab')
The draws below stay inside these ranges and needn't reach their ends.
Inputs may be any that keep to these rules, and one draw needn't show every extreme that they name: obs_cell is local row times 128 plus local column within the observation's region rows and its index of slab's columns.
All inputs are finite; a program needn't handle non-finite values.
Results may differ from the reference program's by a relative error of at most 0.0003.
Values sent between devices are 32-bit elements; how exact they have to be, the bound alone decides.
No kernel may reach another device: no remote copies, remote signals or barrier semaphores. Data moves between devices by JAX's collectives and lax.ppermute only.
A program may use at most 64 MiB of HBM per device.

```python
import math
import jax
import jax.numpy as jnp
from jax import lax

LATITUDE_COUNT = 2
CY = 128
OBS_REG = 128
STEPS = 12
SWEEPS = 8
MEMBERS = 8
REGIONS = 8
NX = 16
NY = 512
N_SLAB = 4


def with_ends(array, key, low, high):
    place = [jax.random.randint(jax.random.fold_in(key, axis), (), 0, length) for axis, length in enumerate(array.shape)]
    longest = array.shape.index(max(array.shape))
    beside = place[:longest] + [(place[longest] + 1) % array.shape[longest]] + place[longest + 1:]
    return array.at[tuple(place)].set(low).at[tuple(beside)].set(high)


def level_of(rng, extent, shards, least, largest):
    level = 1.0
    for axis_at, blocks in shards:
        heights = jax.random.uniform(jax.random.fold_in(jax.random.fold_in(rng, 6), axis_at), (blocks,), jnp.float32, least / len(shards), largest / len(shards))
        level = level * jnp.repeat(jnp.exp(heights), extent[axis_at] // blocks).reshape((-1,) + (1,) * (len(extent) - 1 - axis_at))
    return level


def noise(stream_key, dims, scale, limit, cuts=(), kind=jnp.bfloat16):
    result = jax.random.normal(stream_key, dims, jnp.float32) * scale
    if len(cuts) > 0:
        result = level_of(stream_key, dims, cuts, -0.22, 0.18) * result
    return jnp.clip(result, min=-limit, max=limit).astype(kind)


def setup_inputs(seed: int = 0) -> dict:
    arg_keys = jax.random.split(jax.random.key(seed), 5)
    return {
        "prior_sample_stack": noise(arg_keys[0], (MEMBERS, 3, NX, NY), 0.3, 4.0, ((0, 8), (3, 4)), jnp.float32),
        "obs_cell": with_ends(jax.random.randint(arg_keys[1], (REGIONS, N_SLAB * OBS_REG), 0, LATITUDE_COUNT * CY), jax.random.fold_in(arg_keys[1], 1), 0, (LATITUDE_COUNT * CY) - 1).astype(jnp.int32),
        "obs_value": noise(arg_keys[2], (REGIONS, N_SLAB * OBS_REG), 0.5, 4.0, ((0, 8), (1, 4)), jnp.float32),
        "obs_bin": with_ends(jax.random.randint(arg_keys[3], (REGIONS, N_SLAB * OBS_REG), 0, 4), jax.random.fold_in(arg_keys[3], 1), 0, 3).astype(jnp.int32),
    }


time_step = 0.25
gravity = 1.0
mean_depth = 1.0
coriolis = 0.2
viscosity = 0.4
inflation = 1.1
highest = lax.Precision.HIGHEST

def centre(values):
    return values[:, 1:-1]

def east_of(values):
    return jnp.roll(values[:, 1:-1], -1, 0)

def west_of(values):
    return jnp.roll(values[:, 1:-1], 1, 0)

def north_of(values):
    return values[:, 2:]

def south_of(values):
    return values[:, :-2]

def spread(values):
    return east_of(values) + west_of(values) + north_of(values) + south_of(values) - 4.0 * centre(values)

def slope_x(values):
    return 0.5 * (east_of(values) - west_of(values))

def slope_y(values):
    return 0.5 * (north_of(values) - south_of(values))

def advance(padded):
    elevation_anomaly = padded[0]
    east_wind = padded[1]
    north_wind = padded[2]
    flux_x = (mean_depth + elevation_anomaly) * east_wind
    flux_y = (mean_depth + elevation_anomaly) * north_wind
    east_mid = centre(east_wind)
    north_mid = centre(north_wind)
    new_height = centre(elevation_anomaly) + time_step * (viscosity * spread(elevation_anomaly) - slope_x(flux_x) - slope_y(flux_y))
    new_east = east_mid + time_step * (viscosity * spread(east_wind) - east_mid * slope_x(east_wind) - north_mid * slope_y(east_wind) - gravity * slope_x(elevation_anomaly) + coriolis * north_mid)
    new_north = north_mid + time_step * (viscosity * spread(north_wind) - east_mid * slope_x(north_wind) - north_mid * slope_y(north_wind) - gravity * slope_y(elevation_anomaly) - coriolis * east_mid)
    return jnp.stack([new_height, new_east, new_north])

def partial_sums(anomaly, distance, obs_weight, innovation, band_rows):
    target = jnp.arange(band_rows).astype(jnp.float32)
    scaled_dist = (distance[None, :] - target[:, None]) / float(band_rows)
    weight = obs_weight[None, :] * jnp.exp(-0.5 * scaled_dist * scaled_dist)
    scaled = anomaly[None, :, :] * weight[:, None, :]
    gram_matrix = jnp.einsum('tmj,kj->tmk', scaled, anomaly, precision=highest)
    pull_vector = jnp.einsum('tmj,j->tm', scaled, innovation, precision=highest)
    return (gram_matrix, pull_vector)

def batch_product(left, right):
    return jnp.einsum('tij,tjk->tik', left, right, precision=highest)

def weights_from(gram_matrix, pull_vector, members):
    identity = jnp.eye(members, dtype=jnp.float32)
    gram_matrix = gram_matrix + (members - 1) / inflation * identity[None]
    traces = jnp.trace(gram_matrix, axis1=1, axis2=2)
    iterate = gram_matrix / traces[:, None, None]
    inverse = jnp.broadcast_to(identity, gram_matrix.shape)
    for iteration in range(SWEEPS):
        correction = 1.5 * identity[None] - 0.5 * batch_product(inverse, iterate)
        iterate, inverse = (batch_product(iterate, correction), batch_product(correction, inverse))
    inv_root = inverse / jnp.sqrt(traces)[:, None, None]
    inner = jnp.einsum('tij,tj->ti', inv_root, pull_vector, precision=highest)
    mean_weights = jnp.einsum('tij,tj->ti', inv_root, inner, precision=highest)
    return math.sqrt(members - 1) * inv_root + mean_weights[:, :, None]

def apply_weights(zone_portion, mixing):
    mean_state = lax.optimization_barrier(jnp.mean(zone_portion, axis=0))
    spread_state = zone_portion - mean_state[None]
    return mean_state[None] + jnp.einsum('mftc,tmk->kftc', spread_state, mixing, precision=highest)

def realization_prediction(sample_realization):

    def one_step(counter, values):
        padded = jnp.concatenate([values[:, :, -1:], values, values[:, :, :1]], axis=2)
        return advance(padded)
    return lax.fori_loop(0, STEPS, one_step, sample_realization)

def reference(prior_sample_stack, obs_cell, obs_value, obs_bin):
    predicted_grid = lax.map(realization_prediction, prior_sample_stack)
    elevation_anomaly = predicted_grid[:, 0]
    slab_of = (jnp.arange(N_SLAB * OBS_REG) // OBS_REG).astype(jnp.int32)
    region_ids = jnp.arange(REGIONS).astype(jnp.int32)
    obs_rows = region_ids[:, None] * LATITUDE_COUNT + obs_cell // CY
    obs_columns = slab_of[None, :] * CY + obs_cell % CY
    observed = elevation_anomaly[:, obs_rows, obs_columns]
    obs_mean = lax.optimization_barrier(jnp.mean(observed, axis=0))
    anomaly_all = jnp.transpose(observed - obs_mean[None], (1, 0, 2))
    innovation_all = obs_value - obs_mean
    weight_all = 10.0 / (1.0 + obs_bin.astype(jnp.float32))
    local_rows = (obs_cell // CY).astype(jnp.float32)
    offsets = jnp.arange(-2, 3).astype(jnp.int32)

    def analyse(zone_portion_range):
        chosen = (zone_portion_range + offsets) % REGIONS
        anomaly = jnp.moveaxis(anomaly_all[chosen], 0, 1).reshape(MEMBERS, -1)
        distance = ((offsets * LATITUDE_COUNT).astype(jnp.float32)[:, None] + local_rows[chosen]).reshape(-1)
        gram_matrix, pull_vector = partial_sums(anomaly, distance, weight_all[chosen].reshape(-1), innovation_all[chosen].reshape(-1), LATITUDE_COUNT)
        mixing = weights_from(gram_matrix, pull_vector, MEMBERS)
        zone_portion = lax.dynamic_slice_in_dim(predicted_grid, (zone_portion_range * LATITUDE_COUNT).astype(jnp.int32), LATITUDE_COUNT, 2)
        return apply_weights(zone_portion, mixing)
    analysed = lax.map(analyse, region_ids)
    return jnp.transpose(analysed, (1, 2, 0, 3, 4)).reshape(MEMBERS, 3, NX, NY)
```

```python
import math

import jax
import jax.numpy as jnp
from jax import lax
from jax.experimental import pallas as pl
from jax.experimental.pallas import tpu as pltpu
from jax.sharding import PartitionSpec as P

STEPS = 12
SWEEPS = 8


time_step = 0.25
gravity = 1.0
mean_depth = 1.0
coriolis = 0.2
viscosity = 0.4
inflation = 1.1
reach = 2
highest = lax.Precision.HIGHEST


def padded_2(cells, sides, width):
    for axis, dim in sides:
        count = lax.axis_size(axis)
        head = lax.slice_in_dim(cells, 0, width, axis=dim)
        tail = lax.slice_in_dim(cells, cells.shape[dim] - width, cells.shape[dim], axis=dim)
        cells = jnp.concatenate(
            [
                lax.ppermute(tail, axis, [(i, (i + 1) % count) for i in range(count)]),
                cells,
                lax.ppermute(head, axis, [((i + 1) % count, i) for i in range(count)]),
            ],
            axis=dim,
        )
    return cells


def passed_along(value, axis, steps):
    count = lax.axis_size(axis)
    pairs = [(source, (source + steps) % count) for source in range(count)]
    return lax.ppermute(value, axis, pairs)


def centre(values):
    return values[:, 1:-1]


def east_of(values):
    return jnp.roll(values[:, 1:-1], -1, 0)


def west_of(values):
    return jnp.roll(values[:, 1:-1], 1, 0)


def north_of(values):
    return values[:, 2:]


def south_of(values):
    return values[:, :-2]


def spread(values):
    return (
        east_of(values)
        + west_of(values)
        + north_of(values)
        + south_of(values)
        - 4.0 * centre(values)
    )


def slope_x(values):
    return 0.5 * (east_of(values) - west_of(values))


def slope_y(values):
    return 0.5 * (north_of(values) - south_of(values))


def advance(padded):
    elevation_anomaly = padded[0]
    east_wind = padded[1]
    north_wind = padded[2]
    flux_x = (mean_depth + elevation_anomaly) * east_wind
    flux_y = (mean_depth + elevation_anomaly) * north_wind
    east_mid = centre(east_wind)
    north_mid = centre(north_wind)
    new_height = centre(elevation_anomaly) + time_step * (
        viscosity * spread(elevation_anomaly) - slope_x(flux_x) - slope_y(flux_y)
    )
    new_east = east_mid + time_step * (
        viscosity * spread(east_wind)
        - east_mid * slope_x(east_wind)
        - north_mid * slope_y(east_wind)
        - gravity * slope_x(elevation_anomaly)
        + coriolis * north_mid
    )
    new_north = north_mid + time_step * (
        viscosity * spread(north_wind)
        - east_mid * slope_x(north_wind)
        - north_mid * slope_y(north_wind)
        - gravity * slope_y(elevation_anomaly)
        - coriolis * east_mid
    )
    return jnp.stack([new_height, new_east, new_north])


def partial_sums(anomaly, distance, obs_weight, innovation, band_rows):
    target = jnp.arange(band_rows).astype(jnp.float32)
    scaled_dist = (distance[None, :] - target[:, None]) / float(band_rows)
    weight = obs_weight[None, :] * jnp.exp(-0.5 * scaled_dist * scaled_dist)
    scaled = anomaly[None, :, :] * weight[:, None, :]
    gram_matrix = jnp.einsum("tmj,kj->tmk", scaled, anomaly, precision=highest)
    pull_vector = jnp.einsum("tmj,j->tm", scaled, innovation, precision=highest)
    return (gram_matrix, pull_vector)


def batch_product(left, right):
    return jnp.einsum("tij,tjk->tik", left, right, precision=highest)


def weights_from(gram_matrix, pull_vector, members):
    identity = jnp.eye(members, dtype=jnp.float32)
    gram_matrix = gram_matrix + (members - 1) / inflation * identity[None]
    traces = jnp.trace(gram_matrix, axis1=1, axis2=2)
    iterate = gram_matrix / traces[:, None, None]
    inverse = jnp.broadcast_to(identity, gram_matrix.shape)
    for iteration in range(SWEEPS):
        correction = 1.5 * identity[None] - 0.5 * batch_product(inverse, iterate)
        iterate, inverse = (batch_product(iterate, correction), batch_product(correction, inverse))
    inv_root = inverse / jnp.sqrt(traces)[:, None, None]
    inner = jnp.einsum("tij,tj->ti", inv_root, pull_vector, precision=highest)
    mean_weights = jnp.einsum("tij,tj->ti", inv_root, inner, precision=highest)
    return math.sqrt(members - 1) * inv_root + mean_weights[:, :, None]


def apply_weights(zone_portion, mixing):
    mean_state = jnp.mean(zone_portion, axis=0)
    spread_state = zone_portion - mean_state[None]
    return mean_state[None] + jnp.einsum("mftc,tmk->kftc", spread_state, mixing, precision=highest)


def local_general(prior_sample_stack, obs_cell, obs_value, obs_bin):
    current_condition = prior_sample_stack[0]

    def four_steps(counter, values):
        padded = padded_2(values, (("slab", 2),), 4)
        for substep in range(4):
            padded = advance(padded)
        return padded

    current_condition = lax.fori_loop(0, STEPS // 4, four_steps, current_condition)
    predicted_grid = current_condition[None]
    zone_collection = lax.all_to_all(predicted_grid, "mem", split_axis=2, concat_axis=0, tiled=True)
    heights = zone_collection[:, 0]
    members = heights.shape[0]
    band_rows = heights.shape[1]
    columns = heights.shape[2]
    observed = jnp.take(heights.reshape(members, band_rows * columns), obs_cell[0], axis=1)
    obs_mean = jnp.mean(observed, axis=0)
    anomaly = observed - obs_mean[None]
    extras = jnp.stack(
        [
            obs_value[0] - obs_mean,
            10.0 / (1.0 + obs_bin[0].astype(jnp.float32)),
            (obs_cell[0] // columns).astype(jnp.float32),
        ]
    )
    package = (anomaly, extras)
    collected = [(0, package)]
    for stride in (1, -1, 2, -2):
        collected.append((-stride, passed_along((package[0], package[1]), "mem", stride)))
    all_anomaly = jnp.concatenate([entry[1][0] for entry in collected], axis=1)
    distance = jnp.concatenate(
        [entry[1][1][2] + float(entry[0] * band_rows) for entry in collected]
    )
    obs_weight = jnp.concatenate([entry[1][1][1] for entry in collected])
    innovation = jnp.concatenate([entry[1][1][0] for entry in collected])
    gram_matrix, pull_vector = partial_sums(
        all_anomaly, distance, obs_weight, innovation, band_rows
    )
    gram_matrix, pull_vector = lax.psum((gram_matrix, pull_vector), "slab")
    mixing = weights_from(gram_matrix, pull_vector, members)
    return lax.all_to_all(
        apply_weights(zone_collection, mixing), "mem", split_axis=0, concat_axis=2, tiled=True
    )


def pack_kernel(prior_ref, cell_ref, value_ref, bin_ref, pack_ref):
    fields, rows, columns = prior_ref.shape[1:]
    count = cell_ref.shape[1]
    weight = 10.0 / (1.0 + bin_ref[...].astype(jnp.float32))
    both = jnp.concatenate(
        [weight, weight * value_ref[...], jnp.zeros((6, count), jnp.float32)], axis=0
    )
    total = (pack_ref.shape[0] - fields * rows) // 2 * columns
    at_cell = (
        lax.broadcasted_iota(jnp.int32, (total, count), 0) == cell_ref[...]
    ).astype(jnp.float32)
    sums = lax.dot_general(
        both,
        at_cell,
        (((1,), (1,)), ((), ())),
        precision=highest,
        preferred_element_type=jnp.float32,
    )
    for field in range(fields):
        pack_ref[field * rows : (field + 1) * rows, :] = prior_ref[0, field]
    base = fields * rows
    for row in range(total // columns):
        part = slice(row * columns, (row + 1) * columns)
        pack_ref[base + 2 * row : base + 2 * row + 2, :] = sums[0:2, part]


def forecast_kernel(regions, band_rows, *refs):
    pack_refs, out_ref = refs[:-1], refs[-1]
    slabs = len(pack_refs)
    rows = regions * band_rows
    columns = out_ref.shape[1]
    width = slabs * columns

    def field_of(field):
        return [
            jnp.concatenate(
                [ref[pl.ds(field * rows + q, regions, stride=band_rows), :] for ref in pack_refs],
                axis=1,
            )
            for q in range(band_rows)
        ]

    def east(x):
        return [
            x[q + 1] if q + 1 < band_rows else pltpu.roll(x[0], regions - 1, 0)
            for q in range(band_rows)
        ]

    def west(x):
        return [x[q - 1] if q > 0 else pltpu.roll(x[-1], 1, 0) for q in range(band_rows)]

    def north(x):
        return [pltpu.roll(part, width - 1, 1) for part in x]

    def south(x):
        return [pltpu.roll(part, 1, 1) for part in x]

    keep = 1.0 - 4.0 * time_step * viscosity
    blend = time_step * viscosity
    half = 0.5 * time_step
    turn = time_step * coriolis

    def step(counter, state):
        h, u, v = state
        he, hw, hn, hs = east(h), west(h), north(h), south(h)
        ue, uw, un, us = east(u), west(u), north(u), south(u)
        ve, vw, vn, vs = east(v), west(v), north(v), south(v)
        fx = [(mean_depth + a) * b for a, b in zip(h, u)]
        fy = [(mean_depth + a) * b for a, b in zip(h, v)]
        fe, fw, fn, fs = east(fx), west(fx), north(fy), south(fy)
        new_h, new_u, new_v = [], [], []
        for q in range(band_rows):
            new_h.append(
                keep * h[q]
                + blend * ((he[q] + hw[q]) + (hn[q] + hs[q]))
                - half * ((fe[q] - fw[q]) + (fn[q] - fs[q]))
            )
            new_u.append(
                keep * u[q]
                + blend * ((ue[q] + uw[q]) + (un[q] + us[q]))
                - half
                * (
                    u[q] * (ue[q] - uw[q])
                    + v[q] * (un[q] - us[q])
                    + gravity * (he[q] - hw[q])
                )
                + turn * v[q]
            )
            new_v.append(
                keep * v[q]
                + blend * ((ve[q] + vw[q]) + (vn[q] + vs[q]))
                - half
                * (
                    u[q] * (ve[q] - vw[q])
                    + v[q] * (vn[q] - vs[q])
                    + gravity * (hn[q] - hs[q])
                )
                - turn * u[q]
            )
        return new_h, new_u, new_v

    h, u, v = lax.fori_loop(0, STEPS, step, tuple(field_of(field) for field in range(3)))
    at = 0
    for q in range(band_rows):
        for slab in range(slabs):
            out_ref[at : at + regions, :] = h[q][:, slab * columns : (slab + 1) * columns]
            at += regions
    for field in (u, v):
        for q in range(band_rows):
            out_ref[at : at + regions, :] = field[q][:, :columns]
            at += regions
    for q in range(band_rows):
        for ref in pack_refs:
            base = 3 * rows + 2 * q
            out_ref[at : at + 2, :] = ref[base : base + 2, :]
            at += 2


def analysis_kernel(regions, band_rows, slabs, me_ref, *refs):
    members = regions
    pack_refs, out_ref, sums_ref, scratch_ref = refs[:members], refs[-3], refs[-2], refs[-1]
    columns = out_ref.shape[3]
    tall = regions
    h_rows = band_rows * slabs * tall
    f_rows = h_rows + 2 * band_rows * tall
    n_sums = 2 * band_rows * slabs

    me = me_ref[0]
    for b in range(members):
        start = pl.multiple_of((me ^ b) * n_sums, n_sums)
        sums_ref[pl.ds(start, n_sums), :] = pack_refs[b][f_rows : f_rows + n_sums, :]

    lane = lax.broadcasted_iota(jnp.int32, (tall, 128), 1)
    per_row = []
    for q in range(band_rows):
        gram = [[None] * members for _ in range(members)]
        pull = [None] * members
        for slab in range(slabs):
            at = (q * slabs + slab) * tall
            h = [ref[at : at + tall, :] for ref in pack_refs]
            mean = sum(h[1:], h[0]) * (1.0 / members)
            a = [part - mean for part in h]
            k = (q * slabs + slab) * 2
            weight = sums_ref[pl.ds(k, tall, stride=n_sums), :]
            valued = sums_ref[pl.ds(k + 1, tall, stride=n_sums), :]
            left = valued - weight * mean
            for i in range(members):
                wa = weight * a[i]
                for j in range(i, members):
                    term = wa * a[j]
                    gram[i][j] = term if slab == 0 else gram[i][j] + term
                term = left * a[i]
                pull[i] = term if slab == 0 else pull[i] + term
        packed = jnp.zeros((tall, 128), jnp.float32)
        for i in range(members):
            for j in range(i, members):
                value = jnp.sum(gram[i][j], axis=1, keepdims=True)
                here = lane == i * members + j
                if i != j:
                    here = here | (lane == j * members + i)
                packed = jnp.where(here, value, packed)
            value = jnp.sum(pull[i], axis=1, keepdims=True)
            packed = jnp.where(lane == members * members + i, value, packed)
        per_row.append(packed)

    targets = []
    for t in range(band_rows):
        total = None
        for o in range(-reach, reach + 1):
            near = None
            for q in range(band_rows):
                scaled = (o * band_rows + q - t) / float(band_rows)
                term = math.exp(-0.5 * scaled * scaled) * per_row[q]
                near = term if near is None else near + term
            if o % regions:
                near = pltpu.roll(near, (-o) % regions, 0)
            total = near if total is None else total + near
        targets.append(total)
    stacked = jnp.concatenate(targets, axis=0)
    flat_lane = lax.broadcasted_iota(jnp.int32, stacked.shape, 1)
    on_diagonal = (flat_lane < members * members) & (flat_lane % (members + 1) == 0)
    stacked = jnp.where(on_diagonal, stacked + (members - 1) / inflation, stacked)

    turned = jnp.transpose(
        jnp.concatenate(
            [stacked, jnp.zeros((128 - stacked.shape[0], 128), jnp.float32)], axis=0
        )
    )
    gram = [turned[i * members : (i + 1) * members, :] for i in range(members)]
    pull = turned[members * members : members * members + members, :]
    sub = lax.broadcasted_iota(jnp.int32, (members, 128), 0)

    trace = None
    for i in range(members):
        part = gram[i][i : i + 1, :]
        trace = part if trace is None else trace + part
    live = lax.broadcasted_iota(jnp.int32, (1, 128), 1) < stacked.shape[0]
    trace = jnp.where(live, trace, 1.0)
    eye = [jnp.where(sub == i, 1.0, 0.0) for i in range(members)]

    def across(row):
        return jnp.broadcast_to(row, (members, 128))

    def product(left, right):
        result = []
        for i in range(members):
            terms = [across(left[i][k : k + 1, :]) * right[k] for k in range(members)]
            while len(terms) > 1:
                terms = [x + y for x, y in zip(terms[::2], terms[1::2])]
            result.append(terms[0])
        return result

    def applied(matrix, vector):
        terms = [across(vector[k : k + 1, :]) * matrix[k] for k in range(members)]
        while len(terms) > 1:
            terms = [x + y for x, y in zip(terms[::2], terms[1::2])]
        return terms[0]

    scale = 1.0 / trace
    y = [part * across(scale) for part in gram]
    z = None
    for sweep in range(SWEEPS):
        zy = y if z is None else product(z, y)
        k = [1.5 * e - 0.5 * part for e, part in zip(eye, zy)]
        if sweep < SWEEPS - 1:
            y = product(y, k)
            z = k if z is None else product(k, z)

    def rooted(vector):
        return applied(k, applied(z, vector))

    root_scale = lax.rsqrt(trace)
    mean_weight = rooted(rooted(pull)) * across(scale)
    own = rooted(eye[0]) * across(root_scale)
    mixing = math.sqrt(members - 1) * own + mean_weight

    back = jnp.transpose(
        jnp.concatenate([mixing, jnp.zeros((128 - members, 128), jnp.float32)], axis=0)
    )
    for t in range(band_rows):
        part = back[t * regions : (t + 1) * regions, :]
        share = [
            jnp.broadcast_to(part[:, m : m + 1], (regions, columns)) for m in range(members)
        ]
        for field in range(3):
            if field == 0:
                at = t * slabs * tall
            else:
                at = h_rows + ((field - 1) * band_rows + t) * tall
            values = [ref[at : at + tall, :] for ref in pack_refs]
            mean = sum(values[1:], values[0]) * (1.0 / members)
            result = mean
            for m in range(members):
                result = result + (values[m] - mean) * share[m]
            out_ref[0, field, pl.ds(t, regions, stride=band_rows), :] = result


def in_vmem(count):
    return [pl.BlockSpec(memory_space=pltpu.VMEM)] * count


def local_direct(prior_sample_stack, obs_cell, obs_value, obs_bin):
    members = lax.axis_size("mem")
    slabs = lax.axis_size("slab")
    _, fields, rows, columns = prior_sample_stack.shape
    regions = members
    band_rows = rows // regions
    pack = pl.pallas_call(
        pack_kernel,
        out_shape=jax.ShapeDtypeStruct((fields * rows + 2 * band_rows, columns), jnp.float32),
        in_specs=in_vmem(4),
        out_specs=pl.BlockSpec(memory_space=pltpu.VMEM),
    )(prior_sample_stack, obs_cell, obs_value, obs_bin)
    packs = [pack]
    for ahead in range(1, slabs):
        packs.append(lax.ppermute(pack, "slab", [((i + ahead) % slabs, i) for i in range(slabs)]))

    out_rows = band_rows * slabs * regions + 2 * rows + 2 * band_rows * slabs
    block = pl.pallas_call(
        lambda *refs: forecast_kernel(regions, band_rows, *refs),
        out_shape=jax.ShapeDtypeStruct((out_rows, columns), jnp.float32),
        in_specs=in_vmem(slabs),
        out_specs=pl.BlockSpec(memory_space=pltpu.VMEM),
    )(*packs)

    def partner(value, bits):
        return lax.ppermute(value, "mem", [(i, i ^ bits) for i in range(members)])

    blocks = [None] * members
    blocks[0] = block
    for b in range(2, members, 2):
        blocks[b] = partner(block, b)
    for b in range(0, members, 2):
        blocks[b + 1] = partner(blocks[b], 1)

    me = lax.axis_index("mem").astype(jnp.int32).reshape(1)
    return pl.pallas_call(
        lambda *refs: analysis_kernel(regions, band_rows, slabs, *refs),
        out_shape=jax.ShapeDtypeStruct(prior_sample_stack.shape, jnp.float32),
        in_specs=[pl.BlockSpec(memory_space=pltpu.SMEM)] + in_vmem(members),
        out_specs=pl.BlockSpec(memory_space=pltpu.VMEM),
        scratch_shapes=[
            pltpu.VMEM((regions * 2 * band_rows * slabs, columns), jnp.float32),
            pltpu.VMEM((members * members, 128), jnp.float32),
        ],
    )(me, *blocks)


def solution(mesh):
    members, slabs = mesh.shape["mem"], mesh.shape["slab"]

    def local(prior_sample_stack, obs_cell, obs_value, obs_bin):
        _, fields, rows, columns = prior_sample_stack.shape
        power = members & (members - 1) == 0
        small = members * (members + 1) <= 128 and rows <= 128 and members % 8 == 0
        if power and small and columns == 128 and rows % members == 0:
            return local_direct(prior_sample_stack, obs_cell, obs_value, obs_bin)
        return local_general(prior_sample_stack, obs_cell, obs_value, obs_bin)

    placed = (P("mem", None, None, "slab"), P("mem", "slab"), P("mem", "slab"), P("mem", "slab"))
    return jax.shard_map(
        local, mesh=mesh, in_specs=placed, out_specs=P("mem", None, None, "slab"), check_vma=False
    )
```

```python
import math

import jax
import jax.numpy as jnp
from jax import lax
from jax.experimental import pallas as pl
from jax.experimental.pallas import tpu as pltpu
from jax.sharding import PartitionSpec as P

STEPS = 12
SWEEPS = 8


time_step = 0.25
gravity = 1.0
mean_depth = 1.0
coriolis = 0.2
viscosity = 0.4
inflation = 1.1
reach = 2
highest = lax.Precision.HIGHEST


def padded_2(cells, sides, width):
    for axis, dim in sides:
        count = lax.axis_size(axis)
        head = lax.slice_in_dim(cells, 0, width, axis=dim)
        tail = lax.slice_in_dim(cells, cells.shape[dim] - width, cells.shape[dim], axis=dim)
        cells = jnp.concatenate(
            [
                lax.ppermute(tail, axis, [(i, (i + 1) % count) for i in range(count)]),
                cells,
                lax.ppermute(head, axis, [((i + 1) % count, i) for i in range(count)]),
            ],
            axis=dim,
        )
    return cells


def passed_along(value, axis, steps):
    count = lax.axis_size(axis)
    pairs = [(source, (source + steps) % count) for source in range(count)]
    return lax.ppermute(value, axis, pairs)


def centre(values):
    return values[:, 1:-1]


def east_of(values):
    return jnp.roll(values[:, 1:-1], -1, 0)


def west_of(values):
    return jnp.roll(values[:, 1:-1], 1, 0)


def north_of(values):
    return values[:, 2:]


def south_of(values):
    return values[:, :-2]


def spread(values):
    return (
        east_of(values)
        + west_of(values)
        + north_of(values)
        + south_of(values)
        - 4.0 * centre(values)
    )


def slope_x(values):
    return 0.5 * (east_of(values) - west_of(values))


def slope_y(values):
    return 0.5 * (north_of(values) - south_of(values))


def advance(padded):
    elevation_anomaly = padded[0]
    east_wind = padded[1]
    north_wind = padded[2]
    flux_x = (mean_depth + elevation_anomaly) * east_wind
    flux_y = (mean_depth + elevation_anomaly) * north_wind
    east_mid = centre(east_wind)
    north_mid = centre(north_wind)
    new_height = centre(elevation_anomaly) + time_step * (
        viscosity * spread(elevation_anomaly) - slope_x(flux_x) - slope_y(flux_y)
    )
    new_east = east_mid + time_step * (
        viscosity * spread(east_wind)
        - east_mid * slope_x(east_wind)
        - north_mid * slope_y(east_wind)
        - gravity * slope_x(elevation_anomaly)
        + coriolis * north_mid
    )
    new_north = north_mid + time_step * (
        viscosity * spread(north_wind)
        - east_mid * slope_x(north_wind)
        - north_mid * slope_y(north_wind)
        - gravity * slope_y(elevation_anomaly)
        - coriolis * east_mid
    )
    return jnp.stack([new_height, new_east, new_north])


def partial_sums(anomaly, distance, obs_weight, innovation, band_rows):
    target = jnp.arange(band_rows).astype(jnp.float32)
    scaled_dist = (distance[None, :] - target[:, None]) / float(band_rows)
    weight = obs_weight[None, :] * jnp.exp(-0.5 * scaled_dist * scaled_dist)
    scaled = anomaly[None, :, :] * weight[:, None, :]
    gram_matrix = jnp.einsum("tmj,kj->tmk", scaled, anomaly, precision=highest)
    pull_vector = jnp.einsum("tmj,j->tm", scaled, innovation, precision=highest)
    return (gram_matrix, pull_vector)


def batch_product(left, right):
    return jnp.einsum("tij,tjk->tik", left, right, precision=highest)


def weights_from(gram_matrix, pull_vector, members):
    identity = jnp.eye(members, dtype=jnp.float32)
    gram_matrix = gram_matrix + (members - 1) / inflation * identity[None]
    traces = jnp.trace(gram_matrix, axis1=1, axis2=2)
    iterate = gram_matrix / traces[:, None, None]
    inverse = jnp.broadcast_to(identity, gram_matrix.shape)
    for iteration in range(SWEEPS):
        correction = 1.5 * identity[None] - 0.5 * batch_product(inverse, iterate)
        iterate, inverse = (batch_product(iterate, correction), batch_product(correction, inverse))
    inv_root = inverse / jnp.sqrt(traces)[:, None, None]
    inner = jnp.einsum("tij,tj->ti", inv_root, pull_vector, precision=highest)
    mean_weights = jnp.einsum("tij,tj->ti", inv_root, inner, precision=highest)
    return math.sqrt(members - 1) * inv_root + mean_weights[:, :, None]


def apply_weights(zone_portion, mixing):
    mean_state = jnp.mean(zone_portion, axis=0)
    spread_state = zone_portion - mean_state[None]
    return mean_state[None] + jnp.einsum("mftc,tmk->kftc", spread_state, mixing, precision=highest)


def local_general(prior_sample_stack, obs_cell, obs_value, obs_bin):
    current_condition = prior_sample_stack[0]

    def four_steps(counter, values):
        padded = padded_2(values, (("slab", 2),), 4)
        for substep in range(4):
            padded = advance(padded)
        return padded

    current_condition = lax.fori_loop(0, STEPS // 4, four_steps, current_condition)
    predicted_grid = current_condition[None]
    zone_collection = lax.all_to_all(predicted_grid, "mem", split_axis=2, concat_axis=0, tiled=True)
    heights = zone_collection[:, 0]
    members = heights.shape[0]
    band_rows = heights.shape[1]
    columns = heights.shape[2]
    observed = jnp.take(heights.reshape(members, band_rows * columns), obs_cell[0], axis=1)
    obs_mean = jnp.mean(observed, axis=0)
    anomaly = observed - obs_mean[None]
    extras = jnp.stack(
        [
            obs_value[0] - obs_mean,
            10.0 / (1.0 + obs_bin[0].astype(jnp.float32)),
            (obs_cell[0] // columns).astype(jnp.float32),
        ]
    )
    package = (anomaly, extras)
    collected = [(0, package)]
    for stride in (1, -1, 2, -2):
        collected.append((-stride, passed_along((package[0], package[1]), "mem", stride)))
    all_anomaly = jnp.concatenate([entry[1][0] for entry in collected], axis=1)
    distance = jnp.concatenate(
        [entry[1][1][2] + float(entry[0] * band_rows) for entry in collected]
    )
    obs_weight = jnp.concatenate([entry[1][1][1] for entry in collected])
    innovation = jnp.concatenate([entry[1][1][0] for entry in collected])
    gram_matrix, pull_vector = partial_sums(
        all_anomaly, distance, obs_weight, innovation, band_rows
    )
    gram_matrix, pull_vector = lax.psum((gram_matrix, pull_vector), "slab")
    mixing = weights_from(gram_matrix, pull_vector, members)
    return lax.all_to_all(
        apply_weights(zone_collection, mixing), "mem", split_axis=0, concat_axis=2, tiled=True
    )


def pack_kernel(prior_hbm, cell_hbm, value_hbm, bin_hbm, pack_ref, cell_ref, value_ref, bin_ref, sems):
    taken, columns = prior_hbm.shape
    count = cell_hbm.shape[1]
    prior_copy = pltpu.make_async_copy(prior_hbm, pack_ref.at[pl.ds(0, taken), :], sems.at[0])
    copies = [
        pltpu.make_async_copy(source, target, sems.at[1 + i])
        for i, (source, target) in enumerate(
            ((cell_hbm, cell_ref), (value_hbm, value_ref), (bin_hbm, bin_ref))
        )
    ]
    for copy in copies:
        copy.start()
    prior_copy.start()
    for copy in copies:
        copy.wait()
    weight = 10.0 / (1.0 + bin_ref[...].astype(jnp.float32))
    both = jnp.concatenate(
        [weight, weight * value_ref[...], jnp.zeros((6, count), jnp.float32)], axis=0
    )
    total = (pack_ref.shape[0] - taken) // 2 * columns
    at_cell = (
        lax.broadcasted_iota(jnp.int32, (total, count), 0) == cell_ref[...]
    ).astype(jnp.float32)
    sums = lax.dot_general(
        both,
        at_cell,
        (((1,), (1,)), ((), ())),
        precision=highest,
        preferred_element_type=jnp.float32,
    )
    for row in range(total // columns):
        part = slice(row * columns, (row + 1) * columns)
        pack_ref[taken + 2 * row : taken + 2 * row + 2, :] = sums[0:2, part]
    prior_copy.wait()


def forecast_kernel(regions, band_rows, *refs):
    pack_refs, out_ref = refs[:-1], refs[-1]
    slabs = len(pack_refs)
    rows = regions * band_rows
    columns = out_ref.shape[1]
    width = slabs * columns

    def field_of(field):
        return [
            jnp.concatenate(
                [ref[pl.ds(field * rows + q, regions, stride=band_rows), :] for ref in pack_refs],
                axis=1,
            )
            for q in range(band_rows)
        ]

    def east(x):
        return [
            x[q + 1] if q + 1 < band_rows else pltpu.roll(x[0], regions - 1, 0)
            for q in range(band_rows)
        ]

    def west(x):
        return [x[q - 1] if q > 0 else pltpu.roll(x[-1], 1, 0) for q in range(band_rows)]

    def north(x):
        return [pltpu.roll(part, width - 1, 1) for part in x]

    def south(x):
        return [pltpu.roll(part, 1, 1) for part in x]

    keep = 1.0 - 4.0 * time_step * viscosity
    blend = time_step * viscosity
    half = 0.5 * time_step
    turn = time_step * coriolis

    def step(counter, state):
        h, u, v = state
        he, hw, hn, hs = east(h), west(h), north(h), south(h)
        ue, uw, un, us = east(u), west(u), north(u), south(u)
        ve, vw, vn, vs = east(v), west(v), north(v), south(v)
        fx = [(mean_depth + a) * b for a, b in zip(h, u)]
        fy = [(mean_depth + a) * b for a, b in zip(h, v)]
        fe, fw, fn, fs = east(fx), west(fx), north(fy), south(fy)
        new_h, new_u, new_v = [], [], []
        for q in range(band_rows):
            new_h.append(
                keep * h[q]
                + blend * ((he[q] + hw[q]) + (hn[q] + hs[q]))
                - half * ((fe[q] - fw[q]) + (fn[q] - fs[q]))
            )
            new_u.append(
                keep * u[q]
                + blend * ((ue[q] + uw[q]) + (un[q] + us[q]))
                - half
                * (
                    u[q] * (ue[q] - uw[q])
                    + v[q] * (un[q] - us[q])
                    + gravity * (he[q] - hw[q])
                )
                + turn * v[q]
            )
            new_v.append(
                keep * v[q]
                + blend * ((ve[q] + vw[q]) + (vn[q] + vs[q]))
                - half
                * (
                    u[q] * (ve[q] - vw[q])
                    + v[q] * (vn[q] - vs[q])
                    + gravity * (hn[q] - hs[q])
                )
                - turn * u[q]
            )
        return new_h, new_u, new_v

    h, u, v = lax.fori_loop(0, STEPS, step, tuple(field_of(field) for field in range(3)))
    at = 0
    for q in range(band_rows):
        for slab in range(slabs):
            out_ref[at : at + regions, :] = h[q][:, slab * columns : (slab + 1) * columns]
            at += regions
    for field in (u, v):
        for q in range(band_rows):
            out_ref[at : at + regions, :] = field[q][:, :columns]
            at += regions
    for q in range(band_rows):
        for ref in pack_refs:
            base = 3 * rows + 2 * q
            out_ref[at : at + 2, :] = ref[base : base + 2, :]
            at += 2


def analysis_kernel(regions, band_rows, slabs, me_ref, *refs):
    members = regions
    pack_refs, out_ref, sums_ref = refs[:members], refs[-2], refs[-1]
    columns = out_ref.shape[3]
    tall = regions
    h_rows = band_rows * slabs * tall
    f_rows = h_rows + 2 * band_rows * tall
    n_sums = 2 * band_rows * slabs

    me = me_ref[0]
    for b in range(members):
        start = pl.multiple_of((me ^ b) * n_sums, n_sums)
        sums_ref[pl.ds(start, n_sums), :] = pack_refs[b][f_rows : f_rows + n_sums, :]

    lane = lax.broadcasted_iota(jnp.int32, (tall, 128), 1)
    per_row = []
    for q in range(band_rows):
        gram = [[None] * members for _ in range(members)]
        pull = [None] * members
        for slab in range(slabs):
            at = (q * slabs + slab) * tall
            h = [ref[at : at + tall, :] for ref in pack_refs]
            mean = sum(h[1:], h[0]) * (1.0 / members)
            a = [part - mean for part in h]
            k = (q * slabs + slab) * 2
            weight = sums_ref[pl.ds(k, tall, stride=n_sums), :]
            valued = sums_ref[pl.ds(k + 1, tall, stride=n_sums), :]
            left = valued - weight * mean
            for i in range(members):
                wa = weight * a[i]
                for j in range(i, members):
                    term = wa * a[j]
                    gram[i][j] = term if slab == 0 else gram[i][j] + term
                term = left * a[i]
                pull[i] = term if slab == 0 else pull[i] + term
        packed = jnp.zeros((tall, 128), jnp.float32)
        for i in range(members):
            for j in range(i, members):
                value = jnp.sum(gram[i][j], axis=1, keepdims=True)
                here = lane == i * members + j
                if i != j:
                    here = here | (lane == j * members + i)
                packed = jnp.where(here, value, packed)
            value = jnp.sum(pull[i], axis=1, keepdims=True)
            packed = jnp.where(lane == members * members + i, value, packed)
        per_row.append(packed)

    targets = []
    for t in range(band_rows):
        total = None
        for o in range(-reach, reach + 1):
            near = None
            for q in range(band_rows):
                scaled = (o * band_rows + q - t) / float(band_rows)
                term = math.exp(-0.5 * scaled * scaled) * per_row[q]
                near = term if near is None else near + term
            if o % regions:
                near = pltpu.roll(near, (-o) % regions, 0)
            total = near if total is None else total + near
        targets.append(total)
    stacked = jnp.concatenate(targets, axis=0)
    flat_lane = lax.broadcasted_iota(jnp.int32, stacked.shape, 1)
    on_diagonal = (flat_lane < members * members) & (flat_lane % (members + 1) == 0)
    stacked = jnp.where(on_diagonal, stacked + (members - 1) / inflation, stacked)

    turned = jnp.transpose(
        jnp.concatenate(
            [stacked, jnp.zeros((128 - stacked.shape[0], 128), jnp.float32)], axis=0
        )
    )
    gram = [turned[i * members : (i + 1) * members, :] for i in range(members)]
    pull = turned[members * members : members * members + members, :]
    sub = lax.broadcasted_iota(jnp.int32, (members, 128), 0)

    trace = None
    for i in range(members):
        part = gram[i][i : i + 1, :]
        trace = part if trace is None else trace + part
    live = lax.broadcasted_iota(jnp.int32, (1, 128), 1) < stacked.shape[0]
    trace = jnp.where(live, trace, 1.0)
    eye = [jnp.where(sub == i, 1.0, 0.0) for i in range(members)]

    def across(row):
        return jnp.broadcast_to(row, (members, 128))

    def product(left, right):
        result = []
        for i in range(members):
            terms = [across(left[i][k : k + 1, :]) * right[k] for k in range(members)]
            while len(terms) > 1:
                terms = [x + y for x, y in zip(terms[::2], terms[1::2])]
            result.append(terms[0])
        return result

    def applied(matrix, vector):
        terms = [across(vector[k : k + 1, :]) * matrix[k] for k in range(members)]
        while len(terms) > 1:
            terms = [x + y for x, y in zip(terms[::2], terms[1::2])]
        return terms[0]

    scale = 1.0 / trace
    y = [part * across(scale) for part in gram]
    z = None
    for sweep in range(SWEEPS):
        zy = y if z is None else product(z, y)
        k = [1.5 * e - 0.5 * part for e, part in zip(eye, zy)]
        if sweep < SWEEPS - 1:
            y = product(y, k)
            z = k if z is None else product(k, z)

    def rooted(vector):
        return applied(k, applied(z, vector))

    root_scale = lax.rsqrt(trace)
    mean_weight = rooted(rooted(pull)) * across(scale)
    own = rooted(eye[0]) * across(root_scale)
    mixing = math.sqrt(members - 1) * own + mean_weight

    back = jnp.transpose(
        jnp.concatenate([mixing, jnp.zeros((128 - members, 128), jnp.float32)], axis=0)
    )
    for t in range(band_rows):
        part = back[t * regions : (t + 1) * regions, :]
        share = [
            jnp.broadcast_to(part[:, m : m + 1], (regions, columns)) for m in range(members)
        ]
        for field in range(3):
            if field == 0:
                at = t * slabs * tall
            else:
                at = h_rows + ((field - 1) * band_rows + t) * tall
            values = [ref[at : at + tall, :] for ref in pack_refs]
            mean = sum(values[1:], values[0]) * (1.0 / members)
            result = mean
            for m in range(members):
                result = result + (values[m] - mean) * share[m]
            out_ref[0, field, pl.ds(t, regions, stride=band_rows), :] = result


def in_vmem(count):
    return [pl.BlockSpec(memory_space=pltpu.VMEM)] * count


small_grant = pltpu.CompilerParams(vmem_limit_bytes=4 * 1024 * 1024)


def local_direct(prior_sample_stack, obs_cell, obs_value, obs_bin):
    members = lax.axis_size("mem")
    slabs = lax.axis_size("slab")
    _, fields, rows, columns = prior_sample_stack.shape
    regions = members
    band_rows = rows // regions
    pack = pl.pallas_call(
        pack_kernel,
        out_shape=jax.ShapeDtypeStruct((fields * rows + 2 * band_rows, columns), jnp.float32),
        in_specs=[pl.BlockSpec(memory_space=pltpu.HBM)] * 4,
        out_specs=pl.BlockSpec(memory_space=pltpu.VMEM),
        scratch_shapes=[
            pltpu.VMEM(obs_cell.shape, obs_cell.dtype),
            pltpu.VMEM(obs_value.shape, obs_value.dtype),
            pltpu.VMEM(obs_bin.shape, obs_bin.dtype),
            pltpu.SemaphoreType.DMA((4,)),
        ],
        compiler_params=small_grant,
    )(
        *(
            pltpu.with_memory_space_constraint(array, pltpu.HBM)
            for array in (
                prior_sample_stack.reshape(fields * rows, columns),
                obs_cell,
                obs_value,
                obs_bin,
            )
        )
    )
    packs = [pack]
    for ahead in range(1, slabs):
        packs.append(lax.ppermute(pack, "slab", [((i + ahead) % slabs, i) for i in range(slabs)]))

    out_rows = band_rows * slabs * regions + 2 * rows + 2 * band_rows * slabs
    block = pl.pallas_call(
        lambda *refs: forecast_kernel(regions, band_rows, *refs),
        out_shape=jax.ShapeDtypeStruct((out_rows, columns), jnp.float32),
        in_specs=in_vmem(slabs),
        out_specs=pl.BlockSpec(memory_space=pltpu.VMEM),
        compiler_params=small_grant,
    )(*packs)

    def partner(value, bits):
        return lax.ppermute(value, "mem", [(i, i ^ bits) for i in range(members)])

    blocks = [None] * members
    blocks[0] = block
    for b in range(2, members, 2):
        blocks[b] = partner(block, b)
    for b in range(0, members, 2):
        blocks[b + 1] = partner(blocks[b], 1)

    me = lax.axis_index("mem").astype(jnp.int32).reshape(1)
    return pl.pallas_call(
        lambda *refs: analysis_kernel(regions, band_rows, slabs, *refs),
        out_shape=jax.ShapeDtypeStruct(prior_sample_stack.shape, jnp.float32),
        in_specs=[pl.BlockSpec(memory_space=pltpu.SMEM)] + in_vmem(members),
        out_specs=pl.BlockSpec(memory_space=pltpu.VMEM),
        compiler_params=small_grant,
        scratch_shapes=[
            pltpu.VMEM((regions * 2 * band_rows * slabs, columns), jnp.float32),
        ],
    )(me, *blocks)


def solution(mesh):
    members, slabs = mesh.shape["mem"], mesh.shape["slab"]

    def local(prior_sample_stack, obs_cell, obs_value, obs_bin):
        _, fields, rows, columns = prior_sample_stack.shape
        power = members & (members - 1) == 0
        small = members * (members + 1) <= 128 and rows <= 128 and members % 8 == 0
        if power and small and columns == 128 and rows % members == 0:
            return local_direct(prior_sample_stack, obs_cell, obs_value, obs_bin)
        return local_general(prior_sample_stack, obs_cell, obs_value, obs_bin)

    placed = (P("mem", None, None, "slab"), P("mem", "slab"), P("mem", "slab"), P("mem", "slab"))
    return jax.shard_map(
        local, mesh=mesh, in_specs=placed, out_specs=P("mem", None, None, "slab"), check_vma=False
    )
```

```python
import math

import jax
import jax.numpy as jnp
from jax import lax
from jax.experimental import pallas as pl
from jax.experimental.pallas import tpu as pltpu
from jax.sharding import PartitionSpec as P

STEPS = 12
SWEEPS = 8


time_step = 0.25
gravity = 1.0
mean_depth = 1.0
coriolis = 0.2
viscosity = 0.4
inflation = 1.1
reach = 2
beside = 1
highest = lax.Precision.HIGHEST


def padded_2(cells, sides, width):
    for axis, dim in sides:
        count = lax.axis_size(axis)
        head = lax.slice_in_dim(cells, 0, width, axis=dim)
        tail = lax.slice_in_dim(cells, cells.shape[dim] - width, cells.shape[dim], axis=dim)
        cells = jnp.concatenate(
            [
                lax.ppermute(tail, axis, [(i, (i + 1) % count) for i in range(count)]),
                cells,
                lax.ppermute(head, axis, [((i + 1) % count, i) for i in range(count)]),
            ],
            axis=dim,
        )
    return cells


def passed_along(value, axis, steps):
    count = lax.axis_size(axis)
    pairs = [(source, (source + steps) % count) for source in range(count)]
    return lax.ppermute(value, axis, pairs)


def centre(values):
    return values[:, 1:-1]


def east_of(values):
    return jnp.roll(values[:, 1:-1], -1, 0)


def west_of(values):
    return jnp.roll(values[:, 1:-1], 1, 0)


def north_of(values):
    return values[:, 2:]


def south_of(values):
    return values[:, :-2]


def spread(values):
    return (
        east_of(values)
        + west_of(values)
        + north_of(values)
        + south_of(values)
        - 4.0 * centre(values)
    )


def slope_x(values):
    return 0.5 * (east_of(values) - west_of(values))


def slope_y(values):
    return 0.5 * (north_of(values) - south_of(values))


def advance(padded):
    elevation_anomaly = padded[0]
    east_wind = padded[1]
    north_wind = padded[2]
    flux_x = (mean_depth + elevation_anomaly) * east_wind
    flux_y = (mean_depth + elevation_anomaly) * north_wind
    east_mid = centre(east_wind)
    north_mid = centre(north_wind)
    new_height = centre(elevation_anomaly) + time_step * (
        viscosity * spread(elevation_anomaly) - slope_x(flux_x) - slope_y(flux_y)
    )
    new_east = east_mid + time_step * (
        viscosity * spread(east_wind)
        - east_mid * slope_x(east_wind)
        - north_mid * slope_y(east_wind)
        - gravity * slope_x(elevation_anomaly)
        + coriolis * north_mid
    )
    new_north = north_mid + time_step * (
        viscosity * spread(north_wind)
        - east_mid * slope_x(north_wind)
        - north_mid * slope_y(north_wind)
        - gravity * slope_y(elevation_anomaly)
        - coriolis * east_mid
    )
    return jnp.stack([new_height, new_east, new_north])


def partial_sums(anomaly, distance, obs_weight, innovation, band_rows):
    target = jnp.arange(band_rows).astype(jnp.float32)
    scaled_dist = (distance[None, :] - target[:, None]) / float(band_rows)
    weight = obs_weight[None, :] * jnp.exp(-0.5 * scaled_dist * scaled_dist)
    scaled = anomaly[None, :, :] * weight[:, None, :]
    gram_matrix = jnp.einsum("tmj,kj->tmk", scaled, anomaly, precision=highest)
    pull_vector = jnp.einsum("tmj,j->tm", scaled, innovation, precision=highest)
    return (gram_matrix, pull_vector)


def batch_product(left, right):
    return jnp.einsum("tij,tjk->tik", left, right, precision=highest)


def weights_from(gram_matrix, pull_vector, members):
    identity = jnp.eye(members, dtype=jnp.float32)
    gram_matrix = gram_matrix + (members - 1) / inflation * identity[None]
    traces = jnp.trace(gram_matrix, axis1=1, axis2=2)
    iterate = gram_matrix / traces[:, None, None]
    inverse = jnp.broadcast_to(identity, gram_matrix.shape)
    for iteration in range(SWEEPS):
        correction = 1.5 * identity[None] - 0.5 * batch_product(inverse, iterate)
        iterate, inverse = (batch_product(iterate, correction), batch_product(correction, inverse))
    inv_root = inverse / jnp.sqrt(traces)[:, None, None]
    inner = jnp.einsum("tij,tj->ti", inv_root, pull_vector, precision=highest)
    mean_weights = jnp.einsum("tij,tj->ti", inv_root, inner, precision=highest)
    return math.sqrt(members - 1) * inv_root + mean_weights[:, :, None]


def apply_weights(zone_portion, mixing):
    mean_state = jnp.mean(zone_portion, axis=0)
    spread_state = zone_portion - mean_state[None]
    return mean_state[None] + jnp.einsum("mftc,tmk->kftc", spread_state, mixing, precision=highest)


def local_general(prior_sample_stack, obs_cell, obs_value, obs_bin):
    current_condition = prior_sample_stack[0]

    def four_steps(counter, values):
        padded = padded_2(values, (("slab", 2),), 4)
        for substep in range(4):
            padded = advance(padded)
        return padded

    current_condition = lax.fori_loop(0, STEPS // 4, four_steps, current_condition)
    predicted_grid = current_condition[None]
    zone_collection = lax.all_to_all(predicted_grid, "mem", split_axis=2, concat_axis=0, tiled=True)
    heights = zone_collection[:, 0]
    members = heights.shape[0]
    band_rows = heights.shape[1]
    columns = heights.shape[2]
    observed = jnp.take(heights.reshape(members, band_rows * columns), obs_cell[0], axis=1)
    obs_mean = jnp.mean(observed, axis=0)
    anomaly = observed - obs_mean[None]
    extras = jnp.stack(
        [
            obs_value[0] - obs_mean,
            10.0 / (1.0 + obs_bin[0].astype(jnp.float32)),
            (obs_cell[0] // columns).astype(jnp.float32),
        ]
    )
    package = (anomaly, extras)
    collected = [(0, package)]
    for stride in (1, -1, 2, -2):
        collected.append((-stride, passed_along((package[0], package[1]), "mem", stride)))
    all_anomaly = jnp.concatenate([entry[1][0] for entry in collected], axis=1)
    distance = jnp.concatenate(
        [entry[1][1][2] + float(entry[0] * band_rows) for entry in collected]
    )
    obs_weight = jnp.concatenate([entry[1][1][1] for entry in collected])
    innovation = jnp.concatenate([entry[1][1][0] for entry in collected])
    gram_matrix, pull_vector = partial_sums(
        all_anomaly, distance, obs_weight, innovation, band_rows
    )
    gram_matrix, pull_vector = lax.psum((gram_matrix, pull_vector), "slab")
    mixing = weights_from(gram_matrix, pull_vector, members)
    return lax.all_to_all(
        apply_weights(zone_collection, mixing), "mem", split_axis=0, concat_axis=2, tiled=True
    )


def pack_kernel(prior_hbm, cell_hbm, value_hbm, bin_hbm, pack_ref, cell_ref, value_ref, bin_ref, sems):
    taken, columns = prior_hbm.shape
    count = cell_hbm.shape[1]
    prior_copy = pltpu.make_async_copy(prior_hbm, pack_ref.at[pl.ds(0, taken), :], sems.at[0])
    copies = [
        pltpu.make_async_copy(source, target, sems.at[1 + i])
        for i, (source, target) in enumerate(
            ((cell_hbm, cell_ref), (value_hbm, value_ref), (bin_hbm, bin_ref))
        )
    ]
    for copy in copies:
        copy.start()
    prior_copy.start()
    for copy in copies:
        copy.wait()
    weight = 10.0 / (1.0 + bin_ref[...].astype(jnp.float32))
    parts, rest = [], jnp.concatenate([weight, weight * value_ref[...]], axis=0)
    for _ in range(3):
        part = rest.astype(jnp.bfloat16).astype(jnp.float32)
        parts.append(part)
        rest = rest - part
    parts.append(jnp.zeros((2, count), jnp.float32))
    total = (pack_ref.shape[0] - taken) // 2 * columns
    at_cell = lax.broadcasted_iota(jnp.int32, (total, count), 0) == cell_ref[...]
    sums = lax.dot_general(
        jnp.concatenate(parts, axis=0).astype(jnp.bfloat16),
        jnp.where(at_cell, 1.0, 0.0).astype(jnp.bfloat16),
        (((1,), (1,)), ((), ())),
        preferred_element_type=jnp.float32,
    )
    sums = sums[0:2] + (sums[2:4] + sums[4:6])
    for row in range(total // columns):
        part = slice(row * columns, (row + 1) * columns)
        pack_ref[taken + 2 * row : taken + 2 * row + 2, :] = sums[:, part]
    prior_copy.wait()


def forecast_kernel(regions, band_rows, *refs):
    pack_refs, out_ref = refs[:-1], refs[-1]
    slabs = len(pack_refs)
    rows = regions * band_rows
    columns = out_ref.shape[1]
    width = slabs * columns

    def field_of(field):
        return [
            jnp.concatenate(
                [ref[pl.ds(field * rows + q, regions, stride=band_rows), :] for ref in pack_refs],
                axis=1,
            )
            for q in range(band_rows)
        ]

    def east(x):
        return [
            x[q + 1] if q + 1 < band_rows else pltpu.roll(x[0], regions - 1, 0)
            for q in range(band_rows)
        ]

    def west(x):
        return [x[q - 1] if q > 0 else pltpu.roll(x[-1], 1, 0) for q in range(band_rows)]

    def north(x):
        return [pltpu.roll(part, width - 1, 1) for part in x]

    def south(x):
        return [pltpu.roll(part, 1, 1) for part in x]

    keep = 1.0 - 4.0 * time_step * viscosity
    blend = time_step * viscosity
    half = 0.5 * time_step
    turn = time_step * coriolis

    def step(counter, state):
        h, u, v = state
        he, hw, hn, hs = east(h), west(h), north(h), south(h)
        ue, uw, un, us = east(u), west(u), north(u), south(u)
        ve, vw, vn, vs = east(v), west(v), north(v), south(v)
        new_h, new_u, new_v = [], [], []
        for q in range(band_rows):
            ux, uy = ue[q] - uw[q], un[q] - us[q]
            vx, vy = ve[q] - vw[q], vn[q] - vs[q]
            flux_x = mean_depth * ux + (he[q] * ue[q] - hw[q] * uw[q])
            flux_y = mean_depth * vy + (hn[q] * vn[q] - hs[q] * vs[q])
            new_h.append(
                keep * h[q]
                + blend * ((he[q] + hw[q]) + (hn[q] + hs[q]))
                - half * (flux_x + flux_y)
            )
            new_u.append(
                (keep * u[q] + turn * v[q])
                + blend * ((ue[q] + uw[q]) + (un[q] + us[q]))
                - half * ((u[q] * ux + v[q] * uy) + gravity * (he[q] - hw[q]))
            )
            new_v.append(
                (keep * v[q] - turn * u[q])
                + blend * ((ve[q] + vw[q]) + (vn[q] + vs[q]))
                - half * ((u[q] * vx + v[q] * vy) + gravity * (hn[q] - hs[q]))
            )
        return new_h, new_u, new_v

    h, u, v = lax.fori_loop(
        0, STEPS, step, tuple(field_of(field) for field in range(3)), unroll=STEPS
    )
    at = 0
    for q in range(band_rows):
        for slab in range(slabs):
            out_ref[at : at + regions, :] = h[q][:, slab * columns : (slab + 1) * columns]
            at += regions
    for field in (u, v):
        for q in range(band_rows):
            out_ref[at : at + regions, :] = field[q][:, :columns]
            at += regions
    for q in range(band_rows):
        for ref in pack_refs:
            base = 3 * rows + 2 * q
            out_ref[at : at + 2, :] = ref[base : base + 2, :]
            at += 2


def analysis_kernel(order, band_rows, slabs, me_ref, *refs):
    members = regions = len(order)
    pack_refs, out_ref, sums_ref = [refs[order.index(b)] for b in range(members)], refs[-2], refs[-1]
    columns = out_ref.shape[3]
    tall = regions
    h_rows = band_rows * slabs * tall
    f_rows = h_rows + 2 * band_rows * tall
    n_sums = 2 * band_rows * slabs

    me = me_ref[0]
    for b in range(members):
        start = pl.multiple_of((me ^ b ^ beside) * n_sums, n_sums)
        sums_ref[pl.ds(start, n_sums), :] = pack_refs[b][f_rows : f_rows + n_sums, :]

    lane = lax.broadcasted_iota(jnp.int32, (tall, 128), 1)
    per_row = []
    for q in range(band_rows):
        gram = [[None] * members for _ in range(members)]
        pull = [None] * members
        for slab in range(slabs):
            at = (q * slabs + slab) * tall
            h = [ref[at : at + tall, :] for ref in pack_refs]
            mean = sum(h[1:], h[0]) * (1.0 / members)
            a = [part - mean for part in h]
            k = (q * slabs + slab) * 2
            weight = sums_ref[pl.ds(k, tall, stride=n_sums), :]
            valued = sums_ref[pl.ds(k + 1, tall, stride=n_sums), :]
            left = valued - weight * mean
            for i in range(members):
                wa = weight * a[i]
                for j in range(i, members):
                    term = wa * a[j]
                    gram[i][j] = term if slab == 0 else gram[i][j] + term
                term = left * a[i]
                pull[i] = term if slab == 0 else pull[i] + term
        packed = jnp.zeros((tall, 128), jnp.float32)
        for i in range(members):
            for j in range(i, members):
                value = jnp.sum(gram[i][j], axis=1, keepdims=True)
                here = lane == i * members + j
                if i != j:
                    here = here | (lane == j * members + i)
                packed = jnp.where(here, value, packed)
            value = jnp.sum(pull[i], axis=1, keepdims=True)
            packed = jnp.where(lane == members * members + i, value, packed)
        per_row.append(packed)

    targets = []
    for t in range(band_rows):
        total = None
        for o in range(-reach, reach + 1):
            near = None
            for q in range(band_rows):
                scaled = (o * band_rows + q - t) / float(band_rows)
                term = math.exp(-0.5 * scaled * scaled) * per_row[q]
                near = term if near is None else near + term
            if o % regions:
                near = pltpu.roll(near, (-o) % regions, 0)
            total = near if total is None else total + near
        targets.append(total)
    stacked = jnp.concatenate(targets, axis=0)
    flat_lane = lax.broadcasted_iota(jnp.int32, stacked.shape, 1)
    on_diagonal = (flat_lane < members * members) & (flat_lane % (members + 1) == 0)
    stacked = jnp.where(on_diagonal, stacked + (members - 1) / inflation, stacked)

    turned = jnp.transpose(
        jnp.concatenate(
            [stacked, jnp.zeros((128 - stacked.shape[0], 128), jnp.float32)], axis=0
        )
    )
    gram = [turned[i * members : (i + 1) * members, :] for i in range(members)]
    pull = turned[members * members : members * members + members, :]
    sub = lax.broadcasted_iota(jnp.int32, (members, 128), 0)

    trace = None
    for i in range(members):
        part = gram[i][i : i + 1, :]
        trace = part if trace is None else trace + part
    live = lax.broadcasted_iota(jnp.int32, (1, 128), 1) < stacked.shape[0]
    trace = jnp.where(live, trace, 1.0)
    eye = [jnp.where(sub == i, 1.0, 0.0) for i in range(members)]

    def across(row):
        return jnp.broadcast_to(row, (members, 128))

    def product(left, right):
        result = []
        for i in range(members):
            terms = [across(left[i][k : k + 1, :]) * right[k] for k in range(members)]
            while len(terms) > 1:
                terms = [x + y for x, y in zip(terms[::2], terms[1::2])]
            result.append(terms[0])
        return result

    def applied(matrix, vector):
        terms = [across(vector[k : k + 1, :]) * matrix[k] for k in range(members)]
        while len(terms) > 1:
            terms = [x + y for x, y in zip(terms[::2], terms[1::2])]
        return terms[0]

    scale = 1.0 / trace
    y = [part * across(scale) for part in gram]
    z = None
    for sweep in range(SWEEPS):
        zy = y if z is None else product(z, y)
        k = [1.5 * e - 0.5 * part for e, part in zip(eye, zy)]
        if sweep < SWEEPS - 1:
            y = product(y, k)
            z = k if z is None else product(k, z)

    def rooted(vector):
        return applied(k, applied(z, vector))

    root_scale = lax.rsqrt(trace)
    mean_weight = rooted(rooted(pull)) * across(scale)
    own = rooted(eye[beside]) * across(root_scale)
    mixing = math.sqrt(members - 1) * own + mean_weight

    back = jnp.transpose(
        jnp.concatenate([mixing, jnp.zeros((128 - members, 128), jnp.float32)], axis=0)
    )
    for t in range(band_rows):
        part = back[t * regions : (t + 1) * regions, :]
        share = [
            jnp.broadcast_to(part[:, m : m + 1], (regions, columns)) for m in range(members)
        ]
        for field in range(3):
            if field == 0:
                at = t * slabs * tall
            else:
                at = h_rows + ((field - 1) * band_rows + t) * tall
            values = [ref[at : at + tall, :] for ref in pack_refs]
            mean = sum(values[1:], values[0]) * (1.0 / members)
            result = mean
            for m in range(members):
                result = result + (values[m] - mean) * share[m]
            out_ref[0, field, pl.ds(t, regions, stride=band_rows), :] = result


def in_vmem(count):
    return [pl.BlockSpec(memory_space=pltpu.VMEM)] * count


small_grant = pltpu.CompilerParams(vmem_limit_bytes=4 * 1024 * 1024)


def local_direct(prior_sample_stack, obs_cell, obs_value, obs_bin):
    members = lax.axis_size("mem")
    slabs = lax.axis_size("slab")
    _, fields, rows, columns = prior_sample_stack.shape
    regions = members
    band_rows = rows // regions
    pack = pl.pallas_call(
        pack_kernel,
        out_shape=jax.ShapeDtypeStruct((fields * rows + 2 * band_rows, columns), jnp.float32),
        in_specs=[pl.BlockSpec(memory_space=pltpu.HBM)] * 4,
        out_specs=pl.BlockSpec(memory_space=pltpu.VMEM),
        scratch_shapes=[
            pltpu.VMEM(obs_cell.shape, obs_cell.dtype),
            pltpu.VMEM(obs_value.shape, obs_value.dtype),
            pltpu.VMEM(obs_bin.shape, obs_bin.dtype),
            pltpu.SemaphoreType.DMA((4,)),
        ],
        compiler_params=small_grant,
    )(
        *(
            pltpu.with_memory_space_constraint(array, pltpu.HBM)
            for array in (
                prior_sample_stack.reshape(fields * rows, columns),
                obs_cell,
                obs_value,
                obs_bin,
            )
        )
    )
    packs = [
        lax.ppermute(
            pack,
            ("mem", "slab"),
            [
                ((m ^ beside) * slabs + (s + ahead) % slabs, m * slabs + s)
                for m in range(members)
                for s in range(slabs)
            ],
        )
        for ahead in range(slabs)
    ]

    out_rows = band_rows * slabs * regions + 2 * rows + 2 * band_rows * slabs
    block = pl.pallas_call(
        lambda *refs: forecast_kernel(regions, band_rows, *refs),
        out_shape=jax.ShapeDtypeStruct((out_rows, columns), jnp.float32),
        in_specs=in_vmem(slabs),
        out_specs=pl.BlockSpec(memory_space=pltpu.VMEM),
        compiler_params=small_grant,
    )(*packs)

    def partner(value, bits):
        return lax.ppermute(value, "mem", [(i, i ^ bits) for i in range(members)])

    blocks = {0: block, 1: partner(block, 1)}
    order = [0, 1]
    for b in range(2, members, 2):
        blocks[b + 1] = partner(block, b + 1)
        blocks[b] = partner(block, b) if b == 2 else partner(blocks[b + 1], 1)
        order += [b + 1, b]

    me = lax.axis_index("mem").astype(jnp.int32).reshape(1)
    return pl.pallas_call(
        lambda *refs: analysis_kernel(order, band_rows, slabs, *refs),
        out_shape=jax.ShapeDtypeStruct(prior_sample_stack.shape, jnp.float32),
        in_specs=[pl.BlockSpec(memory_space=pltpu.SMEM)] + in_vmem(members),
        out_specs=pl.BlockSpec(memory_space=pltpu.VMEM),
        compiler_params=small_grant,
        scratch_shapes=[
            pltpu.VMEM((regions * 2 * band_rows * slabs, columns), jnp.float32),
        ],
    )(me, *[blocks[b] for b in order])


def solution(mesh):
    members, slabs = mesh.shape["mem"], mesh.shape["slab"]

    def local(prior_sample_stack, obs_cell, obs_value, obs_bin):
        _, fields, rows, columns = prior_sample_stack.shape
        power = members & (members - 1) == 0
        small = members * (members + 1) <= 128 and rows <= 128 and members % 8 == 0
        if power and small and columns == 128 and rows % members == 0:
            return local_direct(prior_sample_stack, obs_cell, obs_value, obs_bin)
        return local_general(prior_sample_stack, obs_cell, obs_value, obs_bin)

    placed = (P("mem", None, None, "slab"), P("mem", "slab"), P("mem", "slab"), P("mem", "slab"))
    return jax.shard_map(
        local, mesh=mesh, in_specs=placed, out_specs=P("mem", None, None, "slab"), check_vma=False
    )
```

```python
import math

import jax
import jax.numpy as jnp
from jax import lax
from jax.experimental import pallas as pl
from jax.experimental.pallas import tpu as pltpu
from jax.sharding import PartitionSpec as P

STEPS = 12
SWEEPS = 8


time_step = 0.25
gravity = 1.0
mean_depth = 1.0
coriolis = 0.2
viscosity = 0.4
inflation = 1.1
reach = 2
beside = 1
highest = lax.Precision.HIGHEST


def padded_2(cells, sides, width):
    for axis, dim in sides:
        count = lax.axis_size(axis)
        head = lax.slice_in_dim(cells, 0, width, axis=dim)
        tail = lax.slice_in_dim(cells, cells.shape[dim] - width, cells.shape[dim], axis=dim)
        cells = jnp.concatenate(
            [
                lax.ppermute(tail, axis, [(i, (i + 1) % count) for i in range(count)]),
                cells,
                lax.ppermute(head, axis, [((i + 1) % count, i) for i in range(count)]),
            ],
            axis=dim,
        )
    return cells


def passed_along(value, axis, steps):
    count = lax.axis_size(axis)
    pairs = [(source, (source + steps) % count) for source in range(count)]
    return lax.ppermute(value, axis, pairs)


def centre(values):
    return values[:, 1:-1]


def east_of(values):
    return jnp.roll(values[:, 1:-1], -1, 0)


def west_of(values):
    return jnp.roll(values[:, 1:-1], 1, 0)


def north_of(values):
    return values[:, 2:]


def south_of(values):
    return values[:, :-2]


def spread(values):
    return (
        east_of(values)
        + west_of(values)
        + north_of(values)
        + south_of(values)
        - 4.0 * centre(values)
    )


def slope_x(values):
    return 0.5 * (east_of(values) - west_of(values))


def slope_y(values):
    return 0.5 * (north_of(values) - south_of(values))


def advance(padded):
    elevation_anomaly = padded[0]
    east_wind = padded[1]
    north_wind = padded[2]
    flux_x = (mean_depth + elevation_anomaly) * east_wind
    flux_y = (mean_depth + elevation_anomaly) * north_wind
    east_mid = centre(east_wind)
    north_mid = centre(north_wind)
    new_height = centre(elevation_anomaly) + time_step * (
        viscosity * spread(elevation_anomaly) - slope_x(flux_x) - slope_y(flux_y)
    )
    new_east = east_mid + time_step * (
        viscosity * spread(east_wind)
        - east_mid * slope_x(east_wind)
        - north_mid * slope_y(east_wind)
        - gravity * slope_x(elevation_anomaly)
        + coriolis * north_mid
    )
    new_north = north_mid + time_step * (
        viscosity * spread(north_wind)
        - east_mid * slope_x(north_wind)
        - north_mid * slope_y(north_wind)
        - gravity * slope_y(elevation_anomaly)
        - coriolis * east_mid
    )
    return jnp.stack([new_height, new_east, new_north])


def partial_sums(anomaly, distance, obs_weight, innovation, band_rows):
    target = jnp.arange(band_rows).astype(jnp.float32)
    scaled_dist = (distance[None, :] - target[:, None]) / float(band_rows)
    weight = obs_weight[None, :] * jnp.exp(-0.5 * scaled_dist * scaled_dist)
    scaled = anomaly[None, :, :] * weight[:, None, :]
    gram_matrix = jnp.einsum("tmj,kj->tmk", scaled, anomaly, precision=highest)
    pull_vector = jnp.einsum("tmj,j->tm", scaled, innovation, precision=highest)
    return (gram_matrix, pull_vector)


def batch_product(left, right):
    return jnp.einsum("tij,tjk->tik", left, right, precision=highest)


def weights_from(gram_matrix, pull_vector, members):
    identity = jnp.eye(members, dtype=jnp.float32)
    gram_matrix = gram_matrix + (members - 1) / inflation * identity[None]
    traces = jnp.trace(gram_matrix, axis1=1, axis2=2)
    iterate = gram_matrix / traces[:, None, None]
    inverse = jnp.broadcast_to(identity, gram_matrix.shape)
    for iteration in range(SWEEPS):
        correction = 1.5 * identity[None] - 0.5 * batch_product(inverse, iterate)
        iterate, inverse = (batch_product(iterate, correction), batch_product(correction, inverse))
    inv_root = inverse / jnp.sqrt(traces)[:, None, None]
    inner = jnp.einsum("tij,tj->ti", inv_root, pull_vector, precision=highest)
    mean_weights = jnp.einsum("tij,tj->ti", inv_root, inner, precision=highest)
    return math.sqrt(members - 1) * inv_root + mean_weights[:, :, None]


def apply_weights(zone_portion, mixing):
    mean_state = jnp.mean(zone_portion, axis=0)
    spread_state = zone_portion - mean_state[None]
    return mean_state[None] + jnp.einsum("mftc,tmk->kftc", spread_state, mixing, precision=highest)


def local_general(prior_sample_stack, obs_cell, obs_value, obs_bin):
    current_condition = prior_sample_stack[0]

    def four_steps(counter, values):
        padded = padded_2(values, (("slab", 2),), 4)
        for substep in range(4):
            padded = advance(padded)
        return padded

    current_condition = lax.fori_loop(0, STEPS // 4, four_steps, current_condition)
    predicted_grid = current_condition[None]
    zone_collection = lax.all_to_all(predicted_grid, "mem", split_axis=2, concat_axis=0, tiled=True)
    heights = zone_collection[:, 0]
    members = heights.shape[0]
    band_rows = heights.shape[1]
    columns = heights.shape[2]
    observed = jnp.take(heights.reshape(members, band_rows * columns), obs_cell[0], axis=1)
    obs_mean = jnp.mean(observed, axis=0)
    anomaly = observed - obs_mean[None]
    extras = jnp.stack(
        [
            obs_value[0] - obs_mean,
            10.0 / (1.0 + obs_bin[0].astype(jnp.float32)),
            (obs_cell[0] // columns).astype(jnp.float32),
        ]
    )
    package = (anomaly, extras)
    collected = [(0, package)]
    for stride in (1, -1, 2, -2):
        collected.append((-stride, passed_along((package[0], package[1]), "mem", stride)))
    all_anomaly = jnp.concatenate([entry[1][0] for entry in collected], axis=1)
    distance = jnp.concatenate(
        [entry[1][1][2] + float(entry[0] * band_rows) for entry in collected]
    )
    obs_weight = jnp.concatenate([entry[1][1][1] for entry in collected])
    innovation = jnp.concatenate([entry[1][1][0] for entry in collected])
    gram_matrix, pull_vector = partial_sums(
        all_anomaly, distance, obs_weight, innovation, band_rows
    )
    gram_matrix, pull_vector = lax.psum((gram_matrix, pull_vector), "slab")
    mixing = weights_from(gram_matrix, pull_vector, members)
    return lax.all_to_all(
        apply_weights(zone_collection, mixing), "mem", split_axis=0, concat_axis=2, tiled=True
    )


def by_class(lane, columns, slabs):
    width = columns // slabs
    return slabs * (lane % width) + lane // width


def own_part(parts, lane):
    slabs = len(parts)
    result = None
    for w, part in enumerate(parts):
        taken = jnp.take_along_axis(part, lane // slabs, axis=1)
        result = taken if w == 0 else jnp.where(lane % slabs == w, taken, result)
    return result


def pack_kernel(slabs, prior_hbm, cell_hbm, value_hbm, bin_hbm, pack_ref, prior_ref, cell_ref, value_ref, bin_ref, sems):
    taken, columns = prior_hbm.shape
    count = cell_hbm.shape[1]
    prior_copy = pltpu.make_async_copy(prior_hbm, prior_ref, sems.at[0])
    copies = [
        pltpu.make_async_copy(source, target, sems.at[1 + i])
        for i, (source, target) in enumerate(
            ((cell_hbm, cell_ref), (value_hbm, value_ref), (bin_hbm, bin_ref))
        )
    ]
    for copy in copies:
        copy.start()
    prior_copy.start()
    for copy in copies:
        copy.wait()
    weight = 10.0 / (1.0 + bin_ref[...].astype(jnp.float32))
    parts, rest = [], jnp.concatenate([weight, weight * value_ref[...]], axis=0)
    for _ in range(3):
        part = rest.astype(jnp.bfloat16).astype(jnp.float32)
        parts.append(part)
        rest = rest - part
    parts.append(jnp.zeros((2, count), jnp.float32))
    total = (pack_ref.shape[0] - taken) // 2 * columns
    at = lax.broadcasted_iota(jnp.int32, (total, count), 0)
    at_cell = at // columns * columns + by_class(at % columns, columns, slabs) == cell_ref[...]
    sums = lax.dot_general(
        jnp.concatenate(parts, axis=0).astype(jnp.bfloat16),
        jnp.where(at_cell, 1.0, 0.0).astype(jnp.bfloat16),
        (((1,), (1,)), ((), ())),
        preferred_element_type=jnp.float32,
    )
    sums = sums[0:2] + (sums[2:4] + sums[4:6])
    for row in range(total // columns):
        part = slice(row * columns, (row + 1) * columns)
        pack_ref[taken + 2 * row : taken + 2 * row + 2, :] = sums[:, part]
    place = by_class(lax.broadcasted_iota(jnp.int32, (8, columns), 1), columns, slabs)
    prior_copy.wait()
    for row in range(0, taken, 8):
        pack_ref[row : row + 8, :] = jnp.take_along_axis(prior_ref[row : row + 8, :], place, axis=1)


def forecast_kernel(regions, band_rows, *refs):
    pack_refs, out_ref = refs[:-1], refs[-1]
    slabs = len(pack_refs)
    rows = regions * band_rows
    columns = out_ref.shape[1]
    width = columns // slabs

    def interleaved(parts):
        block = lax.broadcasted_iota(jnp.int32, parts[0].shape, 1) // width

        def chosen(pick):
            result = pick(0)
            for k in range(1, slabs):
                result = jnp.where(block == k, pick(k), result)
            return result

        turned = []
        for d in range(slabs):
            mixed = chosen(lambda k: parts[(k + d) % slabs])
            turned.append(pltpu.roll(mixed, d * width, 1) if d else mixed)
        return [chosen(lambda p: turned[(p - w) % slabs]) for w in range(slabs)]

    def field_of(field):
        return [
            interleaved(
                [ref[pl.ds(field * rows + q, regions, stride=band_rows), :] for ref in pack_refs]
            )
            for q in range(band_rows)
        ]

    def east(x, q, w):
        return x[q + 1][w] if q + 1 < band_rows else pltpu.roll(x[0][w], regions - 1, 0)

    def west(x, q, w):
        return x[q - 1][w] if q > 0 else pltpu.roll(x[-1][w], 1, 0)

    def north(x, q, w):
        return x[q][w + 1] if w + 1 < slabs else pltpu.roll(x[q][0], columns - 1, 1)

    def south(x, q, w):
        return x[q][w - 1] if w > 0 else pltpu.roll(x[q][-1], 1, 1)

    keep = 1.0 - 4.0 * time_step * viscosity
    blend = time_step * viscosity
    half = 0.5 * time_step
    turn = time_step * coriolis

    def step(counter, state):
        h, u, v = state
        new_h, new_u, new_v = [], [], []
        for q in range(band_rows):
            for row in (new_h, new_u, new_v):
                row.append([])
            for w in range(slabs):
                sides = [
                    [side(x, q, w) for side in (east, west, north, south)] for x in (h, u, v)
                ]
                (he, hw, hn, hs), (ue, uw, un, us), (ve, vw, vn, vs) = sides
                hm, um, vm = h[q][w], u[q][w], v[q][w]
                ux, uy = ue - uw, un - us
                vx, vy = ve - vw, vn - vs
                flux_x = mean_depth * ux + (he * ue - hw * uw)
                flux_y = mean_depth * vy + (hn * vn - hs * vs)
                new_h[q].append(
                    keep * hm + blend * ((he + hw) + (hn + hs)) - half * (flux_x + flux_y)
                )
                new_u[q].append(
                    (keep * um + turn * vm)
                    + blend * ((ue + uw) + (un + us))
                    - half * ((um * ux + vm * uy) + gravity * (he - hw))
                )
                new_v[q].append(
                    (keep * vm - turn * um)
                    + blend * ((ve + vw) + (vn + vs))
                    - half * ((um * vx + vm * vy) + gravity * (hn - hs))
                )
        return new_h, new_u, new_v

    h, u, v = lax.fori_loop(
        0, STEPS, step, tuple(field_of(field) for field in range(3)), unroll=STEPS
    )
    at = 0
    for q in range(band_rows):
        for w in range(slabs):
            out_ref[at : at + regions, :] = h[q][w]
            at += regions
    lane = lax.broadcasted_iota(jnp.int32, (regions, columns), 1)
    for field in (u, v):
        for q in range(band_rows):
            out_ref[at : at + regions, :] = own_part(field[q], lane)
            at += regions
    base = 3 * rows
    sums = interleaved([ref[base : base + 2 * band_rows, :] for ref in pack_refs])
    for q in range(band_rows):
        for w in range(slabs):
            out_ref[at : at + 2, :] = sums[w][2 * q : 2 * q + 2, :]
            at += 2


def analysis_kernel(order, band_rows, slabs, me_ref, *refs):
    members = regions = len(order)
    pack_refs = [refs[order.index(b)] for b in range(members)]
    out_ref, sums_ref, rows_ref = refs[-3:]
    columns = out_ref.shape[3]
    tall = regions
    h_rows = band_rows * slabs * tall
    f_rows = h_rows + 2 * band_rows * tall
    n_sums = 2 * band_rows * slabs

    me = me_ref[0]
    for b in range(members):
        start = pl.multiple_of((me ^ b ^ beside) * n_sums, n_sums)
        sums_ref[pl.ds(start, n_sums), :] = pack_refs[b][f_rows : f_rows + n_sums, :]

    lane = lax.broadcasted_iota(jnp.int32, (tall, 128), 1)
    per_row = []
    for q in range(band_rows):
        gram = [[None] * members for _ in range(members)]
        pull = [None] * members
        for slab in range(slabs):
            at = (q * slabs + slab) * tall
            h = [ref[at : at + tall, :] for ref in pack_refs]
            mean = sum(h[1:], h[0]) * (1.0 / members)
            a = [part - mean for part in h]
            k = (q * slabs + slab) * 2
            weight = sums_ref[pl.ds(k, tall, stride=n_sums), :]
            valued = sums_ref[pl.ds(k + 1, tall, stride=n_sums), :]
            left = valued - weight * mean
            for i in range(members):
                wa = weight * a[i]
                for j in range(i, members):
                    term = wa * a[j]
                    gram[i][j] = term if slab == 0 else gram[i][j] + term
                term = left * a[i]
                pull[i] = term if slab == 0 else pull[i] + term
        packed = jnp.zeros((tall, 128), jnp.float32)
        for i in range(members):
            for j in range(i, members):
                value = jnp.sum(gram[i][j], axis=1, keepdims=True)
                here = lane == i * members + j
                if i != j:
                    here = here | (lane == j * members + i)
                packed = jnp.where(here, value, packed)
            value = jnp.sum(pull[i], axis=1, keepdims=True)
            packed = jnp.where(lane == members * members + i, value, packed)
        per_row.append(packed)

    targets = []
    for t in range(band_rows):
        total = None
        for o in range(-reach, reach + 1):
            near = None
            for q in range(band_rows):
                scaled = (o * band_rows + q - t) / float(band_rows)
                term = math.exp(-0.5 * scaled * scaled) * per_row[q]
                near = term if near is None else near + term
            if o % regions:
                near = pltpu.roll(near, (-o) % regions, 0)
            total = near if total is None else total + near
        targets.append(total)
    stacked = jnp.concatenate(targets, axis=0)
    flat_lane = lax.broadcasted_iota(jnp.int32, stacked.shape, 1)
    on_diagonal = (flat_lane < members * members) & (flat_lane % (members + 1) == 0)
    stacked = jnp.where(on_diagonal, stacked + (members - 1) / inflation, stacked)

    turned = jnp.transpose(stacked)
    wide = turned.shape[1]
    gram = [turned[i * members : (i + 1) * members, :] for i in range(members)]
    pull = turned[members * members : members * members + members, :]
    sub = lax.broadcasted_iota(jnp.int32, (members, wide), 0)

    trace = None
    for i in range(members):
        part = gram[i][i : i + 1, :]
        trace = part if trace is None else trace + part
    eye = [jnp.where(sub == i, 1.0, 0.0) for i in range(members)]

    def across(row):
        return jnp.broadcast_to(row, (members, wide))

    taken = [0]

    def spread_rows(parts):
        base = taken[0]
        taken[0] += len(parts) * members
        for i, part in enumerate(parts):
            rows_ref[base + i * members : base + (i + 1) * members, :] = part
        return [
            [
                across(rows_ref[base + i * members + k : base + i * members + k + 1, :])
                for k in range(members)
            ]
            for i in range(len(parts))
        ]

    def product(left_rows, right):
        result = []
        for i in range(len(left_rows)):
            terms = [left_rows[i][k] * right[k] for k in range(members)]
            while len(terms) > 1:
                terms = [x + y for x, y in zip(terms[::2], terms[1::2])]
            result.append(terms[0])
        return result

    def applied(matrix, vector):
        return product(spread_rows([vector]), matrix)[0]

    scale = 1.0 / trace
    own = eye[beside] * across(lax.rsqrt(trace))
    mean_weight = pull * across(scale)
    e = [one - part * across(scale) for one, part in zip(eye, gram)]
    for sweep in range(SWEEPS):
        k = [one + 0.5 * part for one, part in zip(eye, e)]
        own = applied(k, own)
        if sweep == SWEEPS - 1:
            mean_weight = applied(k, applied(k, mean_weight))
        else:
            square = product(spread_rows(e), e)
            twice = [one + part + 0.25 * more for one, part, more in zip(eye, e, square)]
            mean_weight = applied(twice, mean_weight)
            e = product(
                spread_rows(square), [0.75 * one + 0.25 * part for one, part in zip(eye, e)]
            )
    mixing = math.sqrt(members - 1) * own + mean_weight

    back = jnp.transpose(mixing)
    place = lax.broadcasted_iota(jnp.int32, (regions, columns), 1)
    for t in range(band_rows):
        part = back[t * regions : (t + 1) * regions, :]
        share = [
            jnp.broadcast_to(part[:, m : m + 1], (regions, columns)) for m in range(members)
        ]
        for field in range(3):
            if field == 0:
                starts = [(t * slabs + w) * tall for w in range(slabs)]
            else:
                starts = [h_rows + ((field - 1) * band_rows + t) * tall]
            results = []
            for at in starts:
                values = [ref[at : at + tall, :] for ref in pack_refs]
                mean = sum(values[1:], values[0]) * (1.0 / members)
                result = mean
                for m in range(members):
                    result = result + (values[m] - mean) * share[m]
                results.append(result)
            result = own_part(results, place) if field == 0 else results[0]
            out_ref[0, field, pl.ds(t, regions, stride=band_rows), :] = result


def in_vmem(count):
    return [pl.BlockSpec(memory_space=pltpu.VMEM)] * count


small_grant = pltpu.CompilerParams(vmem_limit_bytes=4 * 1024 * 1024)


def local_direct(prior_sample_stack, obs_cell, obs_value, obs_bin):
    members = lax.axis_size("mem")
    slabs = lax.axis_size("slab")
    _, fields, rows, columns = prior_sample_stack.shape
    regions = members
    band_rows = rows // regions
    pack = pl.pallas_call(
        lambda *refs: pack_kernel(slabs, *refs),
        out_shape=jax.ShapeDtypeStruct((fields * rows + 2 * band_rows, columns), jnp.float32),
        in_specs=[pl.BlockSpec(memory_space=pltpu.HBM)] * 4,
        out_specs=pl.BlockSpec(memory_space=pltpu.VMEM),
        scratch_shapes=[
            pltpu.VMEM((fields * rows, columns), jnp.float32),
            pltpu.VMEM(obs_cell.shape, obs_cell.dtype),
            pltpu.VMEM(obs_value.shape, obs_value.dtype),
            pltpu.VMEM(obs_bin.shape, obs_bin.dtype),
            pltpu.SemaphoreType.DMA((4,)),
        ],
        compiler_params=small_grant,
    )(
        *(
            pltpu.with_memory_space_constraint(array, pltpu.HBM)
            for array in (
                prior_sample_stack.reshape(fields * rows, columns),
                obs_cell,
                obs_value,
                obs_bin,
            )
        )
    )
    packs = [
        lax.ppermute(
            pack,
            ("mem", "slab"),
            [
                ((m ^ beside) * slabs + (s + ahead) % slabs, m * slabs + s)
                for m in range(members)
                for s in range(slabs)
            ],
        )
        for ahead in range(slabs)
    ]

    out_rows = band_rows * slabs * regions + 2 * rows + 2 * band_rows * slabs
    block = pl.pallas_call(
        lambda *refs: forecast_kernel(regions, band_rows, *refs),
        out_shape=jax.ShapeDtypeStruct((out_rows, columns), jnp.float32),
        in_specs=in_vmem(slabs),
        out_specs=pl.BlockSpec(memory_space=pltpu.VMEM),
        compiler_params=small_grant,
    )(*packs)

    def partner(value, bits):
        return lax.ppermute(value, "mem", [(i, i ^ bits) for i in range(members)])

    blocks = {0: block, 1: partner(block, 1)}
    order = [0, 1]
    for b in range(2, members, 2):
        blocks[b + 1] = partner(block, b + 1)
        blocks[b] = partner(block, b) if b == 2 else partner(blocks[b + 1], 1)
        order += [b + 1, b]

    me = lax.axis_index("mem").astype(jnp.int32).reshape(1)
    return pl.pallas_call(
        lambda *refs: analysis_kernel(order, band_rows, slabs, *refs),
        out_shape=jax.ShapeDtypeStruct(prior_sample_stack.shape, jnp.float32),
        in_specs=[pl.BlockSpec(memory_space=pltpu.SMEM)] + in_vmem(members),
        out_specs=pl.BlockSpec(memory_space=pltpu.VMEM),
        compiler_params=small_grant,
        scratch_shapes=[
            pltpu.VMEM((regions * 2 * band_rows * slabs, columns), jnp.float32),
            pltpu.VMEM((2 * SWEEPS * members * (members + 2), rows), jnp.float32),
        ],
    )(me, *[blocks[b] for b in order])


def solution(mesh):
    members, slabs = mesh.shape["mem"], mesh.shape["slab"]

    def local(prior_sample_stack, obs_cell, obs_value, obs_bin):
        _, fields, rows, columns = prior_sample_stack.shape
        power = members & (members - 1) == 0
        small = members * (members + 1) <= 128 and rows <= 128 and members % 8 == 0
        fits = columns == 128 and columns % slabs == 0 and rows % members == 0
        if power and small and fits:
            return local_direct(prior_sample_stack, obs_cell, obs_value, obs_bin)
        return local_general(prior_sample_stack, obs_cell, obs_value, obs_bin)

    placed = (P("mem", None, None, "slab"), P("mem", "slab"), P("mem", "slab"), P("mem", "slab"))
    return jax.shard_map(
        local, mesh=mesh, in_specs=placed, out_specs=P("mem", None, None, "slab"), check_vma=False
    )
```
